32 devices in a mesh: parts: 2 (over y), horiz: 4 (over z), depth: 2 (over x), comp: 2 (over core).
Axes of the slice: x: 2, y: 2, z: 4, core: 2. Of those that a mesh axis runs over, the one named last changes fastest.
Arguments:
- co2_sat: float32 [1024], P(('parts', 'horiz', 'depth')), parts along dimension 0, may hold values from 0 to 0.8
- pore_press: float32 [1024], P(('parts', 'horiz', 'depth')), parts along dimension 0, may hold values from 0.5 to 1.5
- porosity: float32 [1024], P(('parts', 'horiz', 'depth')), parts along dimension 0, may hold values from 0.05 to 0.3
- facies: int32 [1024], P(('parts', 'horiz', 'depth')), parts along dimension 0, may hold values from 0 to 7
- destination: int32 [1024], P(('parts', 'horiz', 'depth')), parts along dimension 0, may hold values from 0 to 7, as said below
- mineral_mod: float32 [8], replicated, may hold values from 20 to 70
- dry_frac: float32 [8], replicated, may hold values from 0.2 to 0.6
- grain_dens: float32 [8], replicated, may hold values from 2.5 to 2.9
- relax_gain: float32 [8], replicated, may hold values from 0.1 to 0.6
- intersection_item: int32 [4, 32, 32, 128], P(None, ('parts', 'depth'), 'horiz'), parts along dimension 1, may hold values from 0 to 127, as said below
- intersection_weight: float32 [4, 32, 32, 128], P(None, ('parts', 'depth'), 'horiz'), parts along dimension 1, may hold values from 0.1 to 1
- wave_state: float32 [2, 3, 32, 32, 128], P('comp', None, ('parts', 'depth'), 'horiz'), parts along dimension 2, may hold values from -6 to 6
Outputs:
- wave_out: float32 [2, 3, 32, 32, 128], P('comp', None, ('parts', 'depth'), 'horiz'), parts along dimension 2
The draws below stay inside these ranges and needn't reach their ends.
There are 2 independent parts, one for each index of `parts`. The reference program is written for one: setup_inputs(seed, part) draws one part's arguments, and reference() takes and returns one part's arrays. A program takes and returns all parts, laid end to end along the dimension named above; an argument that names none is the same for every part. Nothing has to cross between parts.
Inputs may be any that keep to these rules, and one draw needn't show every extreme that they name: `destination`: each owner's block of 64 cells names every brick at most 16 times. `intersection_item`: every entry s * 16 + j names a reservoir cell of owner s whose destination is the brick of that seismic cell and whose slot_rank is j.
All inputs are finite; a program needn't handle non-finite values.
Results may differ from the reference program's by a relative error of at most 0.0003.
Values sent between devices are 32-bit elements; how exact they have to be, the bound alone decides.
A program may use at most 64 MiB of HBM per device.

```python
import math
import jax
import jax.numpy as jnp
from jax import lax

CX = 8
CZ = 8
NY = 128
STEPS = 4
CAP = 16
FACIES = 8
BRICKS = 8
RES_DEV = 64
RES_TOTAL = 512
NX = 32
NZ = 16
N_DEPTH = 2


def count_table(key):
    base_key = jax.random.fold_in(key, 101)
    hot_key, rows_key = jax.random.split(base_key)
    hottest = jax.random.randint(hot_key, (), 0, BRICKS).astype(jnp.int32)
    live_mean = CAP // 2

    def owner_counts(owner_key):
        order_key, spread_key = jax.random.split(owner_key)
        others = jax.random.permutation(order_key, BRICKS - 1).astype(jnp.int32)
        others = others + (others >= hottest).astype(jnp.int32)
        ordering = jnp.concatenate([hottest[None], others])
        spread = jax.random.randint(spread_key, (BRICKS // 2,), 0, live_mean + 1).astype(jnp.int32)
        spread = spread.at[0].set(live_mean)
        amounts = jnp.stack([live_mean + spread, live_mean - spread], axis=1).reshape(-1)
        return jnp.zeros((BRICKS,), jnp.int32).at[ordering].set(amounts)
    return jax.vmap(owner_counts)(jax.random.split(rows_key, BRICKS))


def draw_destination(key, part):
    counts = count_table(key)
    key = jax.random.fold_in(key, 1)

    def owner_cells(count_row, owner_key):
        listed = jnp.repeat(jnp.arange(BRICKS, dtype=jnp.int32), count_row, total_repeat_length=RES_DEV)
        return jax.random.permutation(owner_key, listed)
    return jax.vmap(owner_cells)(counts, jax.random.split(key, BRICKS)).reshape(-1).astype(jnp.int32)


def draw_intersection_item(key, part):
    counts = count_table(key)
    key = jax.random.fold_in(key, 2)
    by_dest = counts.T.reshape(-1)
    block_ends = jnp.cumsum(by_dest)
    received = jnp.sum(counts, axis=0)
    dest_starts = jnp.cumsum(received) - received
    z_cells = jnp.arange(NZ, dtype=jnp.int32)[:, None]
    x_cells = jnp.arange(NX, dtype=jnp.int32)[None, :]
    brick_id = x_cells // CX * (NZ // CZ) + z_cells // CZ
    item_limit = received[brick_id][None, :, :, None]
    drawn_item = jax.random.randint(key, (4, NZ, NX, NY), 0, item_limit).astype(jnp.int32)
    entry_ids = jnp.arange(4, dtype=jnp.int32)[:, None, None, None]
    y_cells = jnp.arange(NY, dtype=jnp.int32)[None, None, None, :]
    first_cell = (entry_ids == 0) & (z_cells % CZ == 0)[None, :, :, None] & (x_cells % CX == 0)[None, :, :, None] & (y_cells == 0)
    drawn_item = jnp.where(first_cell, item_limit - 1, drawn_item)
    flat_item = dest_starts[brick_id][None, :, :, None] + drawn_item
    block_at = jnp.searchsorted(block_ends, flat_item, side='right').astype(jnp.int32)
    source = block_at % BRICKS
    within = flat_item - (block_ends[block_at] - by_dest[block_at])
    return (source * CAP + within).astype(jnp.int32)


def draw_wave_state(key, part):
    key = jax.random.fold_in(key, 3)
    shape_all = (2, 3, NZ, NX, NY)
    noise_base = jnp.clip(jax.random.normal(key, shape_all, jnp.float32), -6.0, 6.0)
    scales = jnp.array([[0.15, 0.15, 0.15], [1.0, 0.2, 0.2]], jnp.float32)[:, :, None, None, None]
    return (noise_base * scales).astype(jnp.float32)


def plant(entries, own_key, low, high):
    longest = entries.shape.index(max(entries.shape))
    spots = []
    for shift in (0, 1):
        where = [jax.random.randint(jax.random.fold_in(own_key, axis), (), 0, length) for axis, length in enumerate(entries.shape)]
        where[longest] = (where[longest] + shift) % entries.shape[longest]
        spots.append(tuple(where))
    return entries.at[spots[0]].set(low).at[spots[1]].set(high)


def block_scale(stream_key, extent, pieces, least, largest):
    factor_of = 1.0
    for position, parts in pieces:
        steps = jax.random.uniform(jax.random.fold_in(jax.random.fold_in(stream_key, 6), position), (parts,), jnp.float32, least / len(pieces), largest / len(pieces))
        factor_of = factor_of * jnp.repeat(jnp.exp(steps), extent[position] // parts).reshape((-1,) + (1,) * (len(extent) - 1 - position))
    return factor_of


def setup_inputs(seed: int = 0, part: int = 0) -> dict:
    arg_keys = jax.random.split(jax.random.key(seed), 13)
    own_keys = jax.random.split(jax.random.fold_in(arg_keys[12], part), 13)
    co2_sat = jnp.clip(0.8 * jax.random.uniform(own_keys[0], (RES_TOTAL,), jnp.float32) ** block_scale(own_keys[0], (RES_TOTAL,), ((0, 8),), -0.2, 0.2), 0.0, 0.8)
    pore_press = jnp.clip(0.5 + 1.0 * jax.random.uniform(own_keys[1], (RES_TOTAL,), jnp.float32) ** block_scale(own_keys[1], (RES_TOTAL,), ((0, 8),), -0.2, 0.2), 0.5, 1.5)
    porosity = jnp.clip(0.05 + 0.25 * jax.random.uniform(own_keys[2], (RES_TOTAL,), jnp.float32) ** block_scale(own_keys[2], (RES_TOTAL,), ((0, 8),), -0.2, 0.2), 0.05, 0.3)
    facies = plant(jax.random.randint(own_keys[3], (RES_TOTAL,), 0, FACIES), jax.random.fold_in(own_keys[3], 1), 0, FACIES - 1).astype(jnp.int32)
    destination = draw_destination(jax.random.fold_in(jax.random.fold_in(arg_keys[12], part), 71), part)
    mineral_mod = jnp.clip(jnp.exp(jax.random.uniform(arg_keys[5], (FACIES,), jnp.float32, math.log(20.0), math.log(70.0))), 20.0, 70.0)
    dry_frac = jnp.clip(jax.random.uniform(arg_keys[6], (FACIES,), jnp.float32, 0.2, 0.6), 0.2, 0.6)
    grain_dens = jnp.clip(jax.random.uniform(arg_keys[7], (FACIES,), jnp.float32, 2.5, 2.9), 2.5, 2.9)
    relax_gain = jnp.clip(jax.random.uniform(arg_keys[8], (FACIES,), jnp.float32, 0.1, 0.6), 0.1, 0.6)
    intersection_item = draw_intersection_item(jax.random.fold_in(jax.random.fold_in(arg_keys[12], part), 71), part)
    intersection_weight = jnp.clip(jnp.exp(math.log(1.0) - 2.3025851 * jax.random.uniform(own_keys[10], (4, NZ, NX, NY), jnp.float32) ** block_scale(own_keys[10], (4, NZ, NX, NY), ((1, 2), (2, 4)), -0.2, 0.2)), 0.1, 1.0)
    wave_state = draw_wave_state(jax.random.fold_in(jax.random.fold_in(arg_keys[12], part), 71), part)
    return dict(co2_sat=co2_sat, pore_press=pore_press, porosity=porosity, facies=facies, destination=destination, mineral_mod=mineral_mod, dry_frac=dry_frac, grain_dens=grain_dens, relax_gain=relax_gain, intersection_item=intersection_item, intersection_weight=intersection_weight, wave_state=wave_state)


coef_near = 9.0 / 8.0
coef_far = 1.0 / 24.0
courant = 0.08
brine_modulus = 2.5
brine_density = 1.03
gas_density = 0.7
gas_base = 0.02
gas_slope = 0.1
decay_fast = 0.5
decay_slow = 0.9


def shifted(values_in, along_dim, first_index, offset, count_cells):
    return lax.slice_in_dim(values_in, first_index + offset, first_index + offset + count_cells, axis=along_dim)


def forward_diff(values_in, along_dim, first_index, count_cells):
    near_part = shifted(values_in, along_dim, first_index, 1, count_cells) - shifted(values_in, along_dim, first_index, 0, count_cells)
    far_part = shifted(values_in, along_dim, first_index, 2, count_cells) - shifted(values_in, along_dim, first_index, -1, count_cells)
    return coef_near * near_part - coef_far * far_part


def backward_diff(values_in, along_dim, first_index, count_cells):
    near_part = shifted(values_in, along_dim, first_index, 0, count_cells) - shifted(values_in, along_dim, first_index, -1, count_cells)
    far_part = shifted(values_in, along_dim, first_index, 1, count_cells) - shifted(values_in, along_dim, first_index, -2, count_cells)
    return coef_near * near_part - coef_far * far_part


def padded_along(values_in, along_dim, width_cells):
    widths = [(0, 0)] * values_in.ndim
    widths[along_dim] = (width_cells, width_cells)
    return jnp.pad(values_in, widths)


def rock_moduli(saturation, pressure_in, porous, k_min, dry_part, grain_rho, cell_gain):
    water_share = 1.0 - saturation
    k_gas = gas_base + gas_slope * pressure_in
    k_fluid = (brine_modulus - k_gas) * (water_share * water_share * water_share) + k_gas
    k_dry = dry_part * k_min * (1.0 - porous)
    dry_ratio = 1.0 - k_dry / k_min
    denominator = porous / k_fluid + (1.0 - porous) / k_min - k_dry / (k_min * k_min)
    k_sat = k_dry + dry_ratio * dry_ratio / denominator
    density = (1.0 - porous) * grain_rho + porous * (brine_density * water_share + gas_density * saturation)
    return jnp.stack([k_sat, density, cell_gain])


def reference(co2_sat, pore_press, porosity, facies, destination, mineral_mod, dry_frac, grain_dens, relax_gain, intersection_item, intersection_weight, wave_state):
    cell_moduli = rock_moduli(co2_sat, pore_press, porosity, mineral_mod[facies], dry_frac[facies], grain_dens[facies], relax_gain[facies])

    def one_owner(dest_row):
        matches = (dest_row[:, None] == jnp.arange(BRICKS, dtype=jnp.int32)[None, :]).astype(jnp.int32)
        before = jnp.cumsum(matches, axis=0) - matches
        return jnp.sum(before * matches, axis=1).astype(jnp.int32)

    slot_rank = lax.map(one_owner, destination.reshape(BRICKS, RES_DEV)).reshape(-1)
    owner_id = jnp.arange(RES_TOTAL, dtype=jnp.int32) // RES_DEV
    flat_item = (destination * (BRICKS * CAP) + owner_id * CAP + slot_rank).astype(jnp.int32)
    item_table = jnp.ones((3, BRICKS * BRICKS * CAP), jnp.float32).at[:, flat_item].set(cell_moduli)
    brick_id = (jnp.arange(NX, dtype=jnp.int32)[None, :] // CX) * N_DEPTH + jnp.arange(NZ, dtype=jnp.int32)[:, None] // CZ
    offsets = (brick_id * (BRICKS * CAP)).astype(jnp.int32)[:, :, None]
    summed = jnp.zeros((3, NZ, NX, NY), jnp.float32)
    weight_sum = jnp.zeros((NZ, NX, NY), jnp.float32)
    for entry in range(4):
        picked = jnp.take(item_table, (offsets + intersection_item[entry]).astype(jnp.int32), axis=1)
        summed = summed + intersection_weight[entry] * picked
        weight_sum = weight_sum + intersection_weight[entry]
    cell_props = summed / weight_sum
    bulk_modulus, density, memory_gain = cell_props[0], cell_props[1], cell_props[2]

    velocity_z, velocity_x, velocity_y = wave_state[0, 0], wave_state[0, 1], wave_state[0, 2]
    pressure, memory_fast, memory_slow = wave_state[1, 0], wave_state[1, 1], wave_state[1, 2]
    for step_index in range(STEPS):
        velocity_z = velocity_z - courant * forward_diff(padded_along(pressure, 0, 2), 0, 2, NZ) / density
        velocity_x = velocity_x - courant * forward_diff(padded_along(pressure, 1, 2), 1, 2, NX) / density
        velocity_y = velocity_y - courant * forward_diff(padded_along(pressure, 2, 2), 2, 2, NY) / density
        divergence = backward_diff(padded_along(velocity_z, 0, 2), 0, 2, NZ) + backward_diff(padded_along(velocity_x, 1, 2), 1, 2, NX) + backward_diff(padded_along(velocity_y, 2, 2), 2, 2, NY)
        change = courant * bulk_modulus * divergence
        memory_fast = decay_fast * memory_fast + (1.0 - decay_fast) * memory_gain * change
        memory_slow = decay_slow * memory_slow + (1.0 - decay_slow) * memory_gain * change
        pressure = pressure - change + memory_fast + memory_slow
    return jnp.stack([jnp.stack([velocity_z, velocity_x, velocity_y]), jnp.stack([pressure, memory_fast, memory_slow])])
```

```python
import functools

import jax
import jax.numpy as jnp
from jax import lax
from jax.experimental import pallas as pl
from jax.experimental.pallas import tpu as pltpu
from jax.sharding import PartitionSpec as P

STEPS = 4
CAP = 16
LANES = 128
MESH = pl.DeviceIdType.MESH

coef_near = 9.0 / 8.0
coef_far = 1.0 / 24.0
courant = 0.08
brine_modulus = 2.5
brine_density = 1.03
gas_density = 0.7
gas_base = 0.02
gas_slope = 0.1
decay_fast = 0.5
decay_slow = 0.9

SIDES = (("depth", -1), ("depth", 1), ("horiz", -1), ("horiz", 1))
P_LAYERS = 3
V_LAYERS = (1, 2, 1, 2)
MESSAGES = 2 + STEPS - 1


def rock_moduli(saturation, pressure_in, porous, k_min, dry_part, grain_rho):
    water_share = 1.0 - saturation
    k_gas = gas_base + gas_slope * pressure_in
    k_fluid = (brine_modulus - k_gas) * (water_share * water_share * water_share) + k_gas
    k_dry = dry_part * k_min * (1.0 - porous)
    dry_ratio = 1.0 - k_dry / k_min
    denominator = porous / k_fluid + (1.0 - porous) / k_min - k_dry / (k_min * k_min)
    k_sat = k_dry + dry_ratio * dry_ratio / denominator
    density = (1.0 - porous) * grain_rho + porous * (
        brine_density * water_share + gas_density * saturation
    )
    return k_sat, density


def kernel(
    sat_hbm,
    press_hbm,
    poro_hbm,
    facies_hbm,
    dest_hbm,
    mineral_hbm,
    dry_hbm,
    grain_hbm,
    relax_hbm,
    item_hbm,
    weight_hbm,
    state_hbm,
    out_ref,
    cells_f,
    cells_i,
    tables,
    item,
    weight,
    own,
    other,
    table_send,
    table_recv,
    z_send,
    x_send,
    z_recv,
    x_recv,
    p_x,
    v_x,
    rd_x,
    local_sem,
    partner_sem,
    table_send_sem,
    table_recv_sem,
    side_send_sem,
    side_recv_sem,
):
    horiz, depth, comp = (lax.axis_index(a) for a in ("horiz", "depth", "comp"))
    n_horiz, n_depth = lax.axis_size("horiz"), lax.axis_size("depth")
    bricks = n_horiz * n_depth
    me = horiz * n_depth + depth
    cells = dest_hbm.shape[1]
    facies_count = mineral_hbm.shape[0]
    nz, nx, ny = item.shape[1:]
    chunks = table_send.shape[0]
    here = {"depth": depth, "horiz": horiz}
    extent = {"depth": n_depth, "horiz": n_horiz}

    barrier = pltpu.get_barrier_semaphore()

    def brick_id(q):
        return {"horiz": q // n_depth, "depth": lax.rem(q, n_depth)}

    partner = {"comp": 1 - comp}

    z_recv[...] = jnp.zeros_like(z_recv)
    x_recv[...] = jnp.zeros_like(x_recv)

    def each_brick(body):
        if bricks <= 16:
            for d in range(1, bricks):
                body(d)
        else:
            lax.fori_loop(1, bricks, lambda d, c: (body(d), c)[1], 0)

    def greet(d):
        pl.semaphore_signal(
            barrier, inc=1, device_id=brick_id(lax.rem(me + d, bricks)), device_id_type=MESH
        )

    each_brick(greet)
    pl.semaphore_signal(barrier, inc=1, device_id=partner, device_id_type=MESH)

    sources = (
        (sat_hbm, cells_f.at[0]),
        (press_hbm, cells_f.at[1]),
        (poro_hbm, cells_f.at[2]),
        (facies_hbm, cells_i.at[0]),
        (dest_hbm, cells_i.at[1]),
        (mineral_hbm, tables.at[0]),
        (dry_hbm, tables.at[1]),
        (grain_hbm, tables.at[2]),
        (relax_hbm, tables.at[3]),
        (state_hbm.at[0], own),
        (item_hbm, item),
        (weight_hbm, weight),
    )
    loads = [
        pltpu.make_async_copy(src, dst, local_sem.at[k]) for k, (src, dst) in enumerate(sources)
    ]
    for load in loads:
        load.start()
    for load in loads[:9]:
        load.wait()

    facies = cells_i[0]
    drow = cells_i[1]
    picked = []
    for t in range(4):
        row = jnp.zeros(facies.shape, jnp.float32)
        for k in range(facies_count):
            row = jnp.where(facies == k, tables[t, k], row)
        picked.append(row)
    k_sat, rho = rock_moduli(cells_f[0], cells_f[1], cells_f[2], *picked[:3])
    row_id = lax.broadcasted_iota(jnp.int32, (8, cells), 0)
    moduli = jnp.where(
        row_id == 0, k_sat, jnp.where(row_id == 1, rho, jnp.where(row_id == 2, picked[3], 0.0))
    )
    high = moduli.astype(jnp.bfloat16)
    rest = moduli - high.astype(jnp.float32)
    middle = rest.astype(jnp.bfloat16)
    low = (rest - middle.astype(jnp.float32)).astype(jnp.bfloat16)
    pieces = jnp.concatenate(
        [high.astype(jnp.float32), middle.astype(jnp.float32), low.astype(jnp.float32)], axis=0
    ).astype(jnp.bfloat16)
    width = bricks * CAP
    group = min(cells, LANES)
    placed = jnp.zeros((24, width), jnp.float32)
    for first in range(0, cells, group):
        down = lax.broadcasted_iota(jnp.int32, (group, cells), 0) + first
        along = lax.broadcasted_iota(jnp.int32, (group, cells), 1)
        drow_f = drow.astype(jnp.float32)
        spread = jnp.broadcast_to(drow_f, (group, cells))
        dcol = jnp.sum(jnp.where(down == along, spread, 0.0), axis=1, keepdims=True)
        rank = jnp.sum(
            jnp.where((spread == dcol) & (along < down), 1.0, 0.0), axis=1, keepdims=True
        )
        slot = dcol * CAP + rank
        target = lax.broadcasted_iota(jnp.int32, (group, width), 1).astype(jnp.float32)
        place = jnp.where(slot == target, 1.0, 0.0).astype(jnp.bfloat16)
        placed = placed + jnp.dot(
            pieces[:, first : first + group], place, preferred_element_type=jnp.float32
        )
    table = placed[0:8] + placed[8:16] + placed[16:24]
    for c in range(chunks):
        table_send[c] = table[:, c * LANES : (c + 1) * LANES]

    pl.semaphore_wait(barrier, bricks)

    def table_copy(d):
        return pltpu.make_async_remote_copy(
            src_ref=table_send,
            dst_ref=table_recv.at[me],
            send_sem=table_send_sem.at[d],
            recv_sem=table_recv_sem.at[d],
            device_id=brick_id(lax.rem(me + d, bricks)),
            device_id_type=MESH,
        )

    each_brick(lambda d: table_copy(d).start())
    loads[9].wait()
    swap = pltpu.make_async_remote_copy(
        src_ref=own,
        dst_ref=other,
        send_sem=partner_sem.at[0],
        recv_sem=partner_sem.at[1],
        device_id=partner,
        device_id_type=MESH,
    )
    swap.start()
    table_recv[me] = table_send[...]

    def side_copy(message, side, rows):
        axis, step = SIDES[side]
        send, recv = (z_send, z_recv) if axis == "depth" else (x_send, x_recv)
        mine, theirs = side % 2, (side % 2) ^ 1
        return pltpu.make_async_remote_copy(
            src_ref=send.at[message, mine, pl.ds(0, rows)],
            dst_ref=recv.at[message, theirs, pl.ds(0, rows)],
            send_sem=side_send_sem.at[message, side],
            recv_sem=side_recv_sem.at[message, side ^ 1],
            device_id={axis: here[axis] + step},
            device_id_type=MESH,
        )

    def rows_of(message, side):
        if message == 0:
            return P_LAYERS + V_LAYERS[side]
        return V_LAYERS[side] if message == 1 else P_LAYERS

    def exists(side):
        axis, step = SIDES[side]
        place = here[axis] + step
        return (place >= 0) & (place < extent[axis])

    def start_sides(message):
        for side in range(4):

            @pl.when(exists(side))
            def _(side=side):
                side_copy(message, side, rows_of(message, side)).start()

    def wait_sides(message):
        for side in range(4):

            @pl.when(exists(side))
            def _(side=side):
                side_copy(message, side ^ 1, rows_of(message, side ^ 1)).wait_recv()

    def wait_sent(message):
        for side in range(4):

            @pl.when(exists(side))
            def _(side=side):
                side_copy(message, side, rows_of(message, side)).wait_send()

    def pack(message, first, along_z, along_x, layers_low, layers_high):
        z_send[message, 0, first : first + layers_low] = along_z[0:layers_low]
        z_send[message, 1, first : first + layers_high] = along_z[nz - layers_high :]
        for k in range(layers_low):
            x_send[message, 0, first + k] = along_x[:, k, :]
        for k in range(layers_high):
            x_send[message, 1, first + k] = along_x[:, nx - layers_high + k, :]

    lane = lax.broadcasted_iota(jnp.int32, (nz, nx, ny), 2)

    def moved_y(f, offset):
        rolled = pltpu.roll(f, (-offset) % ny, 2)
        keep = lane < ny - offset if offset > 0 else lane >= -offset
        return jnp.where(keep, rolled, 0.0)

    def forward(f0, f1, f2, fm1):
        return coef_near * (f1 - f0) - coef_far * (f2 - fm1)

    def backward(f0, fm1, f1, fm2):
        return coef_near * (f0 - fm1) - coef_far * (f1 - fm2)

    swap.wait_recv()
    first_core = comp == 0
    velocity = [jnp.where(first_core, own[k], other[k]) for k in range(3)]
    pressure, memory_fast, memory_slow = (
        jnp.where(first_core, other[k], own[k]) for k in range(3)
    )
    pack(0, 0, pressure, pressure, P_LAYERS, P_LAYERS)
    pack(0, P_LAYERS, velocity[0], velocity[1], 1, 2)
    start_sides(0)

    each_brick(lambda d: table_copy(d).wait_recv())
    lane_row = lax.broadcasted_iota(jnp.int32, (8, LANES), 1)
    per = LANES // CAP
    my_chunk, my_lane = me // per, lax.rem(me, per) * CAP
    item_rows = []
    for c in range(chunks):
        total = jnp.zeros((8, LANES), jnp.float32)
        for k in range(per):
            tile = table_recv[c * per + k, my_chunk]
            turned = pltpu.roll(tile, lax.rem(k * CAP - my_lane + LANES, LANES), 1)
            total = jnp.where((lane_row >= k * CAP) & (lane_row < (k + 1) * CAP), turned, total)
        item_rows.append(total)

    loads[10].wait()
    loads[11].wait()

    def lookup(r, index):
        found = jnp.zeros((nx, ny), jnp.float32)
        for c in range(chunks):
            source = jnp.broadcast_to(item_rows[c][r : r + 1], (nx, LANES))
            got = jnp.take_along_axis(
                source, lax.rem(index, LANES), axis=1, mode="promise_in_bounds"
            )
            found = got if chunks == 1 else jnp.where(index // LANES == c, got, found)
        return found

    def remap(r):
        return jnp.stack(
            [
                sum(weight[e, z] * lookup(r, item[e, z]) for e in range(4))
                for z in range(nz)
            ]
        )

    weight_sum = weight[0] + weight[1] + weight[2] + weight[3]
    rd = courant * weight_sum / remap(1)
    pack(1, 0, rd, rd, 1, 2)
    start_sides(1)
    bulk = courant * remap(0) / weight_sum
    gain = remap(2) / weight_sum
    gain_fast = (1.0 - decay_fast) * gain
    gain_slow = (1.0 - decay_slow) * gain

    def fill_p(message):
        for k in range(P_LAYERS):
            p_x[:, k, :] = x_recv[message, 0, k]
            p_x[:, P_LAYERS + nx + k, :] = x_recv[message, 1, k]

    span = v_x.shape[1]
    v_x[...] = jnp.zeros_like(v_x)
    rd_x[...] = jnp.zeros_like(rd_x)
    p_x[...] = jnp.zeros_like(p_x)

    wait_sides(0)
    v_x[:, 2 : 2 + nx, :] = velocity[1]
    for k in range(2):
        v_x[:, k, :] = x_recv[0, 0, P_LAYERS + k]
    v_x[:, 2 + nx, :] = x_recv[0, 1, P_LAYERS]
    vz_low, vz_high = z_recv[0, 0, P_LAYERS : P_LAYERS + 2], z_recv[0, 1, P_LAYERS : P_LAYERS + 1]
    v_z = jnp.concatenate([vz_low, velocity[0], vz_high], axis=0)
    v_y = velocity[2]
    rd_x[:, 2 : 2 + nx, :] = rd

    for step in range(STEPS):
        message = 0 if step == 0 else 1 + step
        p_x[:, P_LAYERS : P_LAYERS + nx, :] = pressure
        v_y = v_y - rd * forward(
            pressure, moved_y(pressure, 1), moved_y(pressure, 2), moved_y(pressure, -1)
        )
        part_y = backward(v_y, moved_y(v_y, -1), moved_y(v_y, 1), moved_y(v_y, -2))
        if step == 0:
            wait_sides(1)
            for k in range(2):
                rd_x[:, k, :] = x_recv[1, 0, k]
            rd_x[:, 2 + nx, :] = x_recv[1, 1, 0]
            rd_z = jnp.concatenate([z_recv[1, 0, 0:2], rd, z_recv[1, 1, 0:1]], axis=0)
        else:
            wait_sides(message)
        fill_p(message)
        p_z = jnp.concatenate(
            [z_recv[message, 0, 0:P_LAYERS], pressure, z_recv[message, 1, 0:P_LAYERS]], axis=0
        )
        n = nz + 3
        v_z = v_z - rd_z * forward(
            p_z[1 : 1 + n], p_z[2 : 2 + n], p_z[3 : 3 + n], p_z[0:n]
        )
        v_x[...] = v_x[...] - rd_x[...] * forward(
            p_x[:, 1 : 1 + span, :],
            p_x[:, 2 : 2 + span, :],
            p_x[:, 3 : 3 + span, :],
            p_x[:, 0:span, :],
        )
        part_z = backward(
            v_z[2 : 2 + nz], v_z[1 : 1 + nz], v_z[3 : 3 + nz], v_z[0:nz]
        )
        part_x = backward(
            v_x[:, 2 : 2 + nx, :],
            v_x[:, 1 : 1 + nx, :],
            v_x[:, 3 : 3 + nx, :],
            v_x[:, 0:nx, :],
        )
        change = bulk * (part_z + part_x + part_y)
        memory_fast = decay_fast * memory_fast + gain_fast * change
        memory_slow = decay_slow * memory_slow + gain_slow * change
        pressure = pressure - change + memory_fast + memory_slow
        if step < STEPS - 1:
            pack(2 + step, 0, pressure, pressure, P_LAYERS, P_LAYERS)
            start_sides(2 + step)

    out_ref[0, 0] = jnp.where(first_core, v_z[2 : 2 + nz], pressure)
    out_ref[0, 1] = jnp.where(first_core, v_x[:, 2 : 2 + nx, :], memory_fast)
    out_ref[0, 2] = jnp.where(first_core, v_y, memory_slow)

    each_brick(lambda d: table_copy(d).wait_send())
    swap.wait_send()
    for message in range(MESSAGES):
        wait_sent(message)


def per_device(
    co2_sat,
    pore_press,
    porosity,
    facies,
    destination,
    mineral_mod,
    dry_frac,
    grain_dens,
    relax_gain,
    intersection_item,
    intersection_weight,
    wave_state,
):
    bricks = lax.axis_size(("horiz", "depth"))
    cells = destination.shape[0]
    nz, nx, ny = intersection_item.shape[1:]
    chunks = bricks * CAP // LANES
    span = 8 * -(-(nx + 3) // 8)
    layers = P_LAYERS + 2
    rows = [v.reshape(1, cells) for v in (co2_sat, pore_press, porosity, facies, destination)]
    f32 = jnp.float32
    return pl.pallas_call(
        kernel,
        out_shape=jax.ShapeDtypeStruct(wave_state.shape, f32),
        in_specs=[pl.BlockSpec(memory_space=pl.ANY)] * 12,
        out_specs=pl.BlockSpec(memory_space=pltpu.VMEM),
        scratch_shapes=[
            pltpu.VMEM((3, 1, cells), f32),
            pltpu.VMEM((2, 1, cells), jnp.int32),
            pltpu.SMEM((4, mineral_mod.shape[0]), f32),
            pltpu.VMEM(intersection_item.shape, jnp.int32),
            pltpu.VMEM(intersection_weight.shape, f32),
            pltpu.VMEM((3, nz, nx, ny), f32),
            pltpu.VMEM((3, nz, nx, ny), f32),
            pltpu.VMEM((chunks, 8, LANES), f32),
            pltpu.VMEM((bricks, chunks, 8, LANES), f32),
            pltpu.VMEM((MESSAGES, 2, layers, nx, ny), f32),
            pltpu.VMEM((MESSAGES, 2, layers, nz, ny), f32),
            pltpu.VMEM((MESSAGES, 2, layers, nx, ny), f32),
            pltpu.VMEM((MESSAGES, 2, layers, nz, ny), f32),
            pltpu.VMEM((nz, span + 8, ny), f32),
            pltpu.VMEM((nz, span, ny), f32),
            pltpu.VMEM((nz, span, ny), f32),
            pltpu.SemaphoreType.DMA((12,)),
            pltpu.SemaphoreType.DMA((2,)),
            pltpu.SemaphoreType.DMA((bricks,)),
            pltpu.SemaphoreType.DMA((bricks,)),
            pltpu.SemaphoreType.DMA((MESSAGES, 4)),
            pltpu.SemaphoreType.DMA((MESSAGES, 4)),
        ],
        compiler_params=pltpu.CompilerParams(
            collective_id=0, has_side_effects=True, vmem_limit_bytes=48 * 1024 * 1024
        ),
        name="remap_and_steps",
    )(
        *rows,
        mineral_mod,
        dry_frac,
        grain_dens,
        relax_gain,
        intersection_item,
        intersection_weight,
        wave_state,
    )


def solution(mesh):
    in_specs = (
        P(("parts", "horiz", "depth")),
        P(("parts", "horiz", "depth")),
        P(("parts", "horiz", "depth")),
        P(("parts", "horiz", "depth")),
        P(("parts", "horiz", "depth")),
        P(),
        P(),
        P(),
        P(),
        P(None, ("parts", "depth"), "horiz", None),
        P(None, ("parts", "depth"), "horiz", None),
        P("comp", None, ("parts", "depth"), "horiz", None),
    )
    out_specs = P("comp", None, ("parts", "depth"), "horiz", None)
    return jax.shard_map(
        per_device, mesh=mesh, in_specs=in_specs, out_specs=out_specs, check_vma=False
    )
```

```python
import functools

import jax
import jax.numpy as jnp
from jax import lax
from jax.experimental import pallas as pl
from jax.experimental.pallas import tpu as pltpu
from jax.sharding import PartitionSpec as P

STEPS = 4
CAP = 16
LANES = 128
MESH = pl.DeviceIdType.MESH

coef_near = 9.0 / 8.0
coef_far = 1.0 / 24.0
courant = 0.08
brine_modulus = 2.5
brine_density = 1.03
gas_density = 0.7
gas_base = 0.02
gas_slope = 0.1
decay_fast = 0.5
decay_slow = 0.9

SIDES = (("depth", -1), ("depth", 1), ("horiz", -1), ("horiz", 1))
P_LAYERS = 3
V_LAYERS = (1, 2, 1, 2)
MESSAGES = 2 + STEPS - 1


def rock_moduli(saturation, pressure_in, porous, k_min, dry_part, grain_rho):
    water_share = 1.0 - saturation
    k_gas = gas_base + gas_slope * pressure_in
    k_fluid = (brine_modulus - k_gas) * (water_share * water_share * water_share) + k_gas
    k_dry = dry_part * k_min * (1.0 - porous)
    dry_ratio = 1.0 - k_dry / k_min
    denominator = porous / k_fluid + (1.0 - porous) / k_min - k_dry / (k_min * k_min)
    k_sat = k_dry + dry_ratio * dry_ratio / denominator
    density = (1.0 - porous) * grain_rho + porous * (
        brine_density * water_share + gas_density * saturation
    )
    return k_sat, density


def kernel(
    sat_hbm,
    press_hbm,
    poro_hbm,
    facies_hbm,
    dest_hbm,
    mineral_hbm,
    dry_hbm,
    grain_hbm,
    relax_hbm,
    item_hbm,
    weight_hbm,
    state_hbm,
    out_ref,
    cells_f,
    cells_i,
    tables,
    item,
    weight,
    own,
    other,
    table_send,
    table_recv,
    z_send,
    x_send,
    z_recv,
    x_recv,
    p_x,
    v_x,
    rd_x,
    local_sem,
    partner_sem,
    table_send_sem,
    table_recv_sem,
    side_send_sem,
    side_recv_sem,
):
    horiz, depth, comp = (lax.axis_index(a) for a in ("horiz", "depth", "comp"))
    n_horiz, n_depth = lax.axis_size("horiz"), lax.axis_size("depth")
    bricks = n_horiz * n_depth
    me = horiz * n_depth + depth
    cells = dest_hbm.shape[1]
    facies_count = mineral_hbm.shape[0]
    nz, nx, ny = item.shape[1:]
    chunks = table_send.shape[0]
    here = {"depth": depth, "horiz": horiz}
    extent = {"depth": n_depth, "horiz": n_horiz}

    barrier = pltpu.get_barrier_semaphore()

    def brick_id(q):
        return {"horiz": q // n_depth, "depth": lax.rem(q, n_depth)}

    partner = {"comp": 1 - comp}

    def exists(side):
        axis, step = SIDES[side]
        place = here[axis] + step
        return (place >= 0) & (place < extent[axis])

    for side in range(4):

        @pl.when(jnp.logical_not(exists(side)))
        def _(side=side):
            halo = (z_recv, x_recv)[side // 2]
            for message in range(MESSAGES):
                rows = halo.shape[2] if message == 1 else P_LAYERS + 2
                halo[message, side % 2, 0:rows] = jnp.zeros((rows,) + halo.shape[3:], jnp.float32)

    def each_brick(body):
        if bricks <= 16:
            for d in range(1, bricks):
                body(d)
        else:
            lax.fori_loop(1, bricks, lambda d, c: (body(d), c)[1], 0)

    def greet(d):
        pl.semaphore_signal(
            barrier, inc=1, device_id=brick_id(lax.rem(me + d, bricks)), device_id_type=MESH
        )

    each_brick(greet)
    pl.semaphore_signal(barrier, inc=1, device_id=partner, device_id_type=MESH)

    sources = (
        (sat_hbm, cells_f.at[0]),
        (press_hbm, cells_f.at[1]),
        (poro_hbm, cells_f.at[2]),
        (facies_hbm, cells_i.at[0]),
        (dest_hbm, cells_i.at[1]),
        (mineral_hbm, tables.at[0]),
        (dry_hbm, tables.at[1]),
        (grain_hbm, tables.at[2]),
        (relax_hbm, tables.at[3]),
        (state_hbm.at[0], own),
        (item_hbm, item),
        (weight_hbm, weight),
    )
    loads = [
        pltpu.make_async_copy(src, dst, local_sem.at[k]) for k, (src, dst) in enumerate(sources)
    ]
    for load in loads:
        load.start()
    for load in loads[:9]:
        load.wait()

    facies = cells_i[0]
    drow = cells_i[1]
    picked = []
    for t in range(4):
        row = jnp.zeros(facies.shape, jnp.float32)
        for k in range(facies_count):
            row = jnp.where(facies == k, tables[t, k], row)
        picked.append(row)
    k_sat, rho = rock_moduli(cells_f[0], cells_f[1], cells_f[2], *picked[:3])
    row_id = lax.broadcasted_iota(jnp.int32, (8, cells), 0)
    moduli = jnp.where(
        row_id == 0, k_sat, jnp.where(row_id == 1, rho, jnp.where(row_id == 2, picked[3], 0.0))
    )
    high = moduli.astype(jnp.bfloat16)
    rest = moduli - high.astype(jnp.float32)
    middle = rest.astype(jnp.bfloat16)
    low = (rest - middle.astype(jnp.float32)).astype(jnp.bfloat16)
    pieces = jnp.concatenate(
        [high.astype(jnp.float32), middle.astype(jnp.float32), low.astype(jnp.float32)], axis=0
    ).astype(jnp.bfloat16)
    width = bricks * CAP
    group = min(cells, LANES)
    placed = jnp.zeros((24, width), jnp.float32)
    for first in range(0, cells, group):
        down = lax.broadcasted_iota(jnp.int32, (group, cells), 0) + first
        along = lax.broadcasted_iota(jnp.int32, (group, cells), 1)
        drow_f = drow.astype(jnp.float32)
        spread = jnp.broadcast_to(drow_f, (group, cells))
        dcol = jnp.sum(jnp.where(down == along, spread, 0.0), axis=1, keepdims=True)
        rank = jnp.sum(
            jnp.where((spread == dcol) & (along < down), 1.0, 0.0), axis=1, keepdims=True
        )
        slot = dcol * CAP + rank
        target = lax.broadcasted_iota(jnp.int32, (group, width), 1).astype(jnp.float32)
        place = jnp.where(slot == target, 1.0, 0.0).astype(jnp.bfloat16)
        placed = placed + jnp.dot(
            pieces[:, first : first + group], place, preferred_element_type=jnp.float32
        )
    table = placed[0:8] + placed[8:16] + placed[16:24]
    for c in range(chunks):
        table_send[c] = table[:, c * LANES : (c + 1) * LANES]

    pl.semaphore_wait(barrier, bricks)

    def table_copy(d):
        return pltpu.make_async_remote_copy(
            src_ref=table_send,
            dst_ref=table_recv.at[me],
            send_sem=table_send_sem.at[d],
            recv_sem=table_recv_sem.at[d],
            device_id=brick_id(lax.rem(me + d, bricks)),
            device_id_type=MESH,
        )

    each_brick(lambda d: table_copy(d).start())
    loads[9].wait()
    swap = pltpu.make_async_remote_copy(
        src_ref=own,
        dst_ref=other,
        send_sem=partner_sem.at[0],
        recv_sem=partner_sem.at[1],
        device_id=partner,
        device_id_type=MESH,
    )
    swap.start()
    table_recv[me] = table_send[...]

    def side_copy(message, side, rows):
        axis, step = SIDES[side]
        send, recv = (z_send, z_recv) if axis == "depth" else (x_send, x_recv)
        mine, theirs = side % 2, (side % 2) ^ 1
        return pltpu.make_async_remote_copy(
            src_ref=send.at[message, mine, pl.ds(0, rows)],
            dst_ref=recv.at[message, theirs, pl.ds(0, rows)],
            send_sem=side_send_sem.at[message, side],
            recv_sem=side_recv_sem.at[message, side ^ 1],
            device_id={axis: here[axis] + step},
            device_id_type=MESH,
        )

    def rows_of(message, side):
        if message == 0:
            return P_LAYERS + V_LAYERS[side]
        return 8 * V_LAYERS[side] if message == 1 else P_LAYERS

    def start_sides(message):
        for side in range(4):

            @pl.when(exists(side))
            def _(side=side):
                side_copy(message, side, rows_of(message, side)).start()

    def wait_sides(message):
        for side in range(4):

            @pl.when(exists(side))
            def _(side=side):
                side_copy(message, side ^ 1, rows_of(message, side ^ 1)).wait_recv()

    def wait_sent(message):
        for side in range(4):

            @pl.when(exists(side))
            def _(side=side):
                side_copy(message, side, rows_of(message, side)).wait_send()

    def pack(message, first, along_z, along_x, layers_low, layers_high, apart=1):
        for k in range(layers_low):
            z_send[message, 0, first + apart * k] = along_z[k].astype(jnp.float32)
            x_send[message, 0, first + apart * k] = along_x[:, k, :].astype(jnp.float32)
        for k in range(layers_high):
            layer_z, layer_x = nz - layers_high + k, nx - layers_high + k
            z_send[message, 1, first + apart * k] = along_z[layer_z].astype(jnp.float32)
            x_send[message, 1, first + apart * k] = along_x[:, layer_x, :].astype(jnp.float32)

    lane = lax.broadcasted_iota(jnp.int32, (nz, nx, ny), 2)

    def moved_y(f, offset):
        rolled = pltpu.roll(f, (-offset) % ny, 2)
        keep = lane < ny - offset if offset > 0 else lane >= -offset
        return jnp.where(keep, rolled, 0.0)

    def forward(f0, f1, f2, fm1):
        return coef_near * (f1 - f0) - coef_far * (f2 - fm1)

    def backward(f0, fm1, f1, fm2):
        return coef_near * (f0 - fm1) - coef_far * (f1 - fm2)

    loads[10].wait()
    loads[11].wait()
    for e in range(4):
        pack(1, 2 * e, item.at[e], item.at[e], 1, 2, 8)
        pack(1, 2 * e + 1, weight.at[e], weight.at[e], 1, 2, 8)
    start_sides(1)

    swap.wait_recv()
    first_core = comp == 0
    velocity = [jnp.where(first_core, own[k], other[k]) for k in range(3)]
    pressure, memory_fast, memory_slow = (
        jnp.where(first_core, other[k], own[k]) for k in range(3)
    )
    pack(0, 0, pressure, pressure, P_LAYERS, P_LAYERS)
    pack(0, P_LAYERS, velocity[0], velocity[1], 1, 2)
    start_sides(0)

    each_brick(lambda d: table_copy(d).wait_recv())
    lane_row = lax.broadcasted_iota(jnp.int32, (8, LANES), 1)
    per = LANES // CAP

    def brick_table(brick):
        chunk, first = brick // per, lax.rem(brick, per) * CAP
        rows = []
        for c in range(chunks):
            total = jnp.zeros((8, LANES), jnp.float32)
            for k in range(per):
                tile = table_recv[c * per + k, chunk]
                turned = pltpu.roll(tile, lax.rem(k * CAP - first + LANES, LANES), 1)
                total = jnp.where(
                    (lane_row >= k * CAP) & (lane_row < (k + 1) * CAP), turned, total
                )
            rows.append(total)
        return rows

    def lookup(rows, r, index):
        found = jnp.zeros(index.shape, jnp.float32)
        for c in range(chunks):
            source = jnp.broadcast_to(rows[c][r : r + 1], (index.shape[0], LANES))
            got = jnp.take_along_axis(
                source, lax.rem(index, LANES), axis=1, mode="promise_in_bounds"
            )
            found = got if chunks == 1 else jnp.where(index // LANES == c, got, found)
        return found

    own_rows = brick_table(me)

    def remap(r):
        return jnp.stack(
            [
                sum(weight[e, z] * lookup(own_rows, r, item[e, z]) for e in range(4))
                for z in range(nz)
            ]
        )

    weight_sum = weight[0] + weight[1] + weight[2] + weight[3]
    rd = courant * weight_sum / remap(1)
    bulk = courant * remap(0) / weight_sum
    gain = remap(2) / weight_sum
    gain_fast = (1.0 - decay_fast) * gain
    gain_slow = (1.0 - decay_slow) * gain

    def halo_rd(side):
        axis, step = SIDES[side]
        recv = (z_recv, x_recv)[side // 2]
        there = {**here, axis: jnp.where(exists(side), here[axis] + step, here[axis])}
        rows = brick_table(there["horiz"] * n_depth + there["depth"])
        found = []
        for k in range(V_LAYERS[side ^ 1]):
            total, scale = 0.0, 0.0
            for e in range(4):
                index = recv[1, side % 2, 8 * k + 2 * e].astype(jnp.int32)
                share = recv[1, side % 2, 8 * k + 2 * e + 1]
                total = total + share * lookup(rows, 1, index)
                scale = scale + share
            found.append(jnp.where(exists(side), courant * scale / total, 0.0))
        return found

    def fill_p(message):
        for k in range(P_LAYERS):
            p_x[:, k, :] = x_recv[message, 0, k]
            p_x[:, P_LAYERS + nx + k, :] = x_recv[message, 1, k]

    span = v_x.shape[1]
    v_x[...] = jnp.zeros_like(v_x)
    rd_x[...] = jnp.zeros_like(rd_x)
    p_x[...] = jnp.zeros_like(p_x)

    wait_sides(0)
    v_x[:, 2 : 2 + nx, :] = velocity[1]
    for k in range(2):
        v_x[:, k, :] = x_recv[0, 0, P_LAYERS + k]
    v_x[:, 2 + nx, :] = x_recv[0, 1, P_LAYERS]
    vz_low, vz_high = z_recv[0, 0, P_LAYERS : P_LAYERS + 2], z_recv[0, 1, P_LAYERS : P_LAYERS + 1]
    v_z = jnp.concatenate([vz_low, velocity[0], vz_high], axis=0)
    v_y = velocity[2]
    rd_x[:, 2 : 2 + nx, :] = rd

    for step in range(STEPS):
        message = 0 if step == 0 else 1 + step
        p_x[:, P_LAYERS : P_LAYERS + nx, :] = pressure
        v_y = v_y - rd * forward(
            pressure, moved_y(pressure, 1), moved_y(pressure, 2), moved_y(pressure, -1)
        )
        part_y = backward(v_y, moved_y(v_y, -1), moved_y(v_y, 1), moved_y(v_y, -2))
        if step == 0:
            wait_sides(1)
            halos = [halo_rd(side) for side in range(4)]
            for k in range(2):
                rd_x[:, k, :] = halos[2][k]
            rd_x[:, 2 + nx, :] = halos[3][0]
            rd_z = jnp.concatenate([jnp.stack(halos[0]), rd, jnp.stack(halos[1])], axis=0)
        else:
            wait_sides(message)
        fill_p(message)
        p_z = jnp.concatenate(
            [z_recv[message, 0, 0:P_LAYERS], pressure, z_recv[message, 1, 0:P_LAYERS]], axis=0
        )
        n = nz + 3
        v_z = v_z - rd_z * forward(
            p_z[1 : 1 + n], p_z[2 : 2 + n], p_z[3 : 3 + n], p_z[0:n]
        )
        v_x[...] = v_x[...] - rd_x[...] * forward(
            p_x[:, 1 : 1 + span, :],
            p_x[:, 2 : 2 + span, :],
            p_x[:, 3 : 3 + span, :],
            p_x[:, 0:span, :],
        )
        part_z = backward(
            v_z[2 : 2 + nz], v_z[1 : 1 + nz], v_z[3 : 3 + nz], v_z[0:nz]
        )
        part_x = backward(
            v_x[:, 2 : 2 + nx, :],
            v_x[:, 1 : 1 + nx, :],
            v_x[:, 3 : 3 + nx, :],
            v_x[:, 0:nx, :],
        )
        change = bulk * (part_z + part_x + part_y)
        memory_fast = decay_fast * memory_fast + gain_fast * change
        memory_slow = decay_slow * memory_slow + gain_slow * change
        pressure = pressure - change + memory_fast + memory_slow
        if step < STEPS - 1:
            pack(2 + step, 0, pressure, pressure, P_LAYERS, P_LAYERS)
            start_sides(2 + step)

    out_ref[0, 0] = jnp.where(first_core, v_z[2 : 2 + nz], pressure)
    out_ref[0, 1] = jnp.where(first_core, v_x[:, 2 : 2 + nx, :], memory_fast)
    out_ref[0, 2] = jnp.where(first_core, v_y, memory_slow)

    each_brick(lambda d: table_copy(d).wait_send())
    swap.wait_send()
    for message in range(MESSAGES):
        wait_sent(message)


def per_device(
    co2_sat,
    pore_press,
    porosity,
    facies,
    destination,
    mineral_mod,
    dry_frac,
    grain_dens,
    relax_gain,
    intersection_item,
    intersection_weight,
    wave_state,
):
    bricks = lax.axis_size(("horiz", "depth"))
    cells = destination.shape[0]
    nz, nx, ny = intersection_item.shape[1:]
    chunks = bricks * CAP // LANES
    span = 8 * -(-(nx + 3) // 8)
    layers = max(P_LAYERS + 2, 8 * max(V_LAYERS))
    rows = [v.reshape(1, cells) for v in (co2_sat, pore_press, porosity, facies, destination)]
    f32 = jnp.float32
    return pl.pallas_call(
        kernel,
        out_shape=jax.ShapeDtypeStruct(wave_state.shape, f32),
        in_specs=[pl.BlockSpec(memory_space=pltpu.HBM)] * 12,
        out_specs=pl.BlockSpec(memory_space=pltpu.VMEM),
        scratch_shapes=[
            pltpu.VMEM((3, 1, cells), f32),
            pltpu.VMEM((2, 1, cells), jnp.int32),
            pltpu.SMEM((4, mineral_mod.shape[0]), f32),
            pltpu.VMEM(intersection_item.shape, jnp.int32),
            pltpu.VMEM(intersection_weight.shape, f32),
            pltpu.VMEM((3, nz, nx, ny), f32),
            pltpu.VMEM((3, nz, nx, ny), f32),
            pltpu.VMEM((chunks, 8, LANES), f32),
            pltpu.VMEM((bricks, chunks, 8, LANES), f32),
            pltpu.VMEM((MESSAGES, 2, layers, nx, ny), f32),
            pltpu.VMEM((MESSAGES, 2, layers, nz, ny), f32),
            pltpu.VMEM((MESSAGES, 2, layers, nx, ny), f32),
            pltpu.VMEM((MESSAGES, 2, layers, nz, ny), f32),
            pltpu.VMEM((nz, span + 8, ny), f32),
            pltpu.VMEM((nz, span, ny), f32),
            pltpu.VMEM((nz, span, ny), f32),
            pltpu.SemaphoreType.DMA((12,)),
            pltpu.SemaphoreType.DMA((2,)),
            pltpu.SemaphoreType.DMA((bricks,)),
            pltpu.SemaphoreType.DMA((bricks,)),
            pltpu.SemaphoreType.DMA((MESSAGES, 4)),
            pltpu.SemaphoreType.DMA((MESSAGES, 4)),
        ],
        compiler_params=pltpu.CompilerParams(
            collective_id=0, has_side_effects=True, vmem_limit_bytes=55040 * 1024
        ),
        name="remap_and_steps",
    )(
        *rows,
        mineral_mod,
        dry_frac,
        grain_dens,
        relax_gain,
        intersection_item,
        intersection_weight,
        wave_state,
    )


def solution(mesh):
    in_specs = (
        P(("parts", "horiz", "depth")),
        P(("parts", "horiz", "depth")),
        P(("parts", "horiz", "depth")),
        P(("parts", "horiz", "depth")),
        P(("parts", "horiz", "depth")),
        P(),
        P(),
        P(),
        P(),
        P(None, ("parts", "depth"), "horiz", None),
        P(None, ("parts", "depth"), "horiz", None),
        P("comp", None, ("parts", "depth"), "horiz", None),
    )
    out_specs = P("comp", None, ("parts", "depth"), "horiz", None)
    return jax.shard_map(
        per_device, mesh=mesh, in_specs=in_specs, out_specs=out_specs, check_vma=False
    )
```

```python
import functools

import jax
import jax.numpy as jnp
from jax import lax
from jax.experimental import pallas as pl
from jax.experimental.pallas import tpu as pltpu
from jax.sharding import PartitionSpec as P

STEPS = 4
CAP = 16
LANES = 128
MESH = pl.DeviceIdType.MESH

coef_near = 9.0 / 8.0
coef_far = 1.0 / 24.0
courant = 0.08
brine_modulus = 2.5
brine_density = 1.03
gas_density = 0.7
gas_base = 0.02
gas_slope = 0.1
decay_fast = 0.5
decay_slow = 0.9

SIDES = (("depth", -1), ("depth", 1), ("horiz", -1), ("horiz", 1))
P_LAYERS = 3
V_LAYERS = (1, 2, 1, 2)
MESSAGES = 2 + STEPS - 1


def rock_moduli(saturation, pressure_in, porous, k_min, dry_part, grain_rho):
    water_share = 1.0 - saturation
    k_gas = gas_base + gas_slope * pressure_in
    k_fluid = (brine_modulus - k_gas) * (water_share * water_share * water_share) + k_gas
    k_dry = dry_part * k_min * (1.0 - porous)
    dry_ratio = 1.0 - k_dry / k_min
    denominator = porous / k_fluid + (1.0 - porous) / k_min - k_dry / (k_min * k_min)
    k_sat = k_dry + dry_ratio * dry_ratio / denominator
    density = (1.0 - porous) * grain_rho + porous * (
        brine_density * water_share + gas_density * saturation
    )
    return k_sat, density


def kernel(
    sat_hbm,
    press_hbm,
    poro_hbm,
    facies_hbm,
    dest_hbm,
    mineral_hbm,
    dry_hbm,
    grain_hbm,
    relax_hbm,
    item_hbm,
    weight_hbm,
    state_hbm,
    out_ref,
    cells_f,
    cells_i,
    tables,
    item,
    weight,
    own,
    other,
    table_send,
    table_recv,
    z_send,
    x_send,
    z_recv,
    x_recv,
    p_x,
    v_x,
    rd_x,
    local_sem,
    partner_sem,
    table_send_sem,
    table_recv_sem,
    side_send_sem,
    side_recv_sem,
):
    horiz, depth, comp = (lax.axis_index(a) for a in ("horiz", "depth", "comp"))
    n_horiz, n_depth = lax.axis_size("horiz"), lax.axis_size("depth")
    bricks = n_horiz * n_depth
    me = horiz * n_depth + depth
    cells = dest_hbm.shape[1]
    facies_count = mineral_hbm.shape[0]
    nz, nx, ny = item.shape[1:]
    chunks = table_send.shape[0]
    here = {"depth": depth, "horiz": horiz}
    extent = {"depth": n_depth, "horiz": n_horiz}

    barrier = pltpu.get_barrier_semaphore()

    def brick_id(q):
        return {"horiz": q // n_depth, "depth": lax.rem(q, n_depth)}

    partner = {"comp": 1 - comp}

    def exists(side):
        axis, step = SIDES[side]
        place = here[axis] + step
        return (place >= 0) & (place < extent[axis])

    for side in range(4):

        @pl.when(jnp.logical_not(exists(side)))
        def _(side=side):
            halo = (z_recv, x_recv)[side // 2]
            for message in range(MESSAGES):
                rows = halo.shape[2] if message == 1 else P_LAYERS + 2
                halo[message, side % 2, 0:rows] = jnp.zeros((rows,) + halo.shape[3:], jnp.float32)

    def each_brick(body):
        if bricks <= 16:
            for d in range(1, bricks):
                body(d)
        else:
            lax.fori_loop(1, bricks, lambda d, c: (body(d), c)[1], 0)

    def greet(d):
        pl.semaphore_signal(
            barrier, inc=1, device_id=brick_id(lax.rem(me + d, bricks)), device_id_type=MESH
        )

    each_brick(greet)
    pl.semaphore_signal(barrier, inc=1, device_id=partner, device_id_type=MESH)

    sources = (
        (sat_hbm, cells_f.at[0]),
        (press_hbm, cells_f.at[1]),
        (poro_hbm, cells_f.at[2]),
        (facies_hbm, cells_i.at[0]),
        (dest_hbm, cells_i.at[1]),
        (mineral_hbm, tables.at[0]),
        (dry_hbm, tables.at[1]),
        (grain_hbm, tables.at[2]),
        (relax_hbm, tables.at[3]),
        (state_hbm.at[0], own),
        (item_hbm, item),
        (weight_hbm, weight),
    )
    loads = [
        pltpu.make_async_copy(src, dst, local_sem.at[k]) for k, (src, dst) in enumerate(sources)
    ]
    for load in loads:
        load.start()
    for load in loads[:9]:
        load.wait()

    facies = cells_i[0]
    drow = cells_i[1]
    picked = []
    for t in range(4):
        row = jnp.zeros(facies.shape, jnp.float32)
        for k in range(facies_count):
            row = jnp.where(facies == k, tables[t, k], row)
        picked.append(row)
    k_sat, rho = rock_moduli(cells_f[0], cells_f[1], cells_f[2], *picked[:3])
    row_id = lax.broadcasted_iota(jnp.int32, (8, cells), 0)
    moduli = jnp.where(
        row_id == 0, k_sat, jnp.where(row_id == 1, rho, jnp.where(row_id == 2, picked[3], 0.0))
    )
    high = moduli.astype(jnp.bfloat16)
    rest = moduli - high.astype(jnp.float32)
    middle = rest.astype(jnp.bfloat16)
    low = (rest - middle.astype(jnp.float32)).astype(jnp.bfloat16)
    pieces = jnp.concatenate(
        [high.astype(jnp.float32), middle.astype(jnp.float32), low.astype(jnp.float32)], axis=0
    ).astype(jnp.bfloat16)
    width = bricks * CAP
    group = min(cells, LANES)
    placed = jnp.zeros((24, width), jnp.float32)
    for first in range(0, cells, group):
        down = lax.broadcasted_iota(jnp.int32, (group, cells), 0) + first
        along = lax.broadcasted_iota(jnp.int32, (group, cells), 1)
        drow_f = drow.astype(jnp.float32)
        spread = jnp.broadcast_to(drow_f, (group, cells))
        dcol = jnp.sum(jnp.where(down == along, spread, 0.0), axis=1, keepdims=True)
        rank = jnp.sum(
            jnp.where((spread == dcol) & (along < down), 1.0, 0.0), axis=1, keepdims=True
        )
        slot = dcol * CAP + rank
        target = lax.broadcasted_iota(jnp.int32, (group, width), 1).astype(jnp.float32)
        place = jnp.where(slot == target, 1.0, 0.0).astype(jnp.bfloat16)
        placed = placed + jnp.dot(
            pieces[:, first : first + group], place, preferred_element_type=jnp.float32
        )
    table = placed[0:8] + placed[8:16] + placed[16:24]
    for c in range(chunks):
        table_send[c] = table[:, c * LANES : (c + 1) * LANES]

    pl.semaphore_wait(barrier, bricks)

    def table_copy(d):
        return pltpu.make_async_remote_copy(
            src_ref=table_send,
            dst_ref=table_recv.at[me],
            send_sem=table_send_sem.at[d],
            recv_sem=table_recv_sem.at[d],
            device_id=brick_id(lax.rem(me + d, bricks)),
            device_id_type=MESH,
        )

    each_brick(lambda d: table_copy(d).start())
    loads[9].wait()
    swap = pltpu.make_async_remote_copy(
        src_ref=own,
        dst_ref=other,
        send_sem=partner_sem.at[0],
        recv_sem=partner_sem.at[1],
        device_id=partner,
        device_id_type=MESH,
    )
    swap.start()
    table_recv[me] = table_send[...]

    def side_copy(message, side, rows):
        axis, step = SIDES[side]
        send, recv = (z_send, z_recv) if axis == "depth" else (x_send, x_recv)
        mine, theirs = side % 2, (side % 2) ^ 1
        return pltpu.make_async_remote_copy(
            src_ref=send.at[message, mine, pl.ds(0, rows)],
            dst_ref=recv.at[message, theirs, pl.ds(0, rows)],
            send_sem=side_send_sem.at[message, side],
            recv_sem=side_recv_sem.at[message, side ^ 1],
            device_id={axis: here[axis] + step},
            device_id_type=MESH,
        )

    def rows_of(message, side):
        if message == 0:
            return P_LAYERS + V_LAYERS[side]
        return 8 * V_LAYERS[side] if message == 1 else P_LAYERS

    def start_sides(message):
        for side in (2, 3, 0, 1):

            @pl.when(exists(side))
            def _(side=side):
                side_copy(message, side, rows_of(message, side)).start()

    def wait_sides(message, sides=(2, 3, 0, 1)):
        for side in sides:

            @pl.when(exists(side))
            def _(side=side):
                side_copy(message, side ^ 1, rows_of(message, side ^ 1)).wait_recv()

    def wait_sent(message):
        for side in range(4):

            @pl.when(exists(side))
            def _(side=side):
                side_copy(message, side, rows_of(message, side)).wait_send()

    def pack(message, first, along_z, along_x, layers_low, layers_high, apart=1):
        for k in range(layers_low):
            z_send[message, 0, first + apart * k] = along_z[k].astype(jnp.float32)
            x_send[message, 0, first + apart * k] = along_x[:, k, :].astype(jnp.float32)
        for k in range(layers_high):
            layer_z, layer_x = nz - layers_high + k, nx - layers_high + k
            z_send[message, 1, first + apart * k] = along_z[layer_z].astype(jnp.float32)
            x_send[message, 1, first + apart * k] = along_x[:, layer_x, :].astype(jnp.float32)

    lane = lax.broadcasted_iota(jnp.int32, (nz, nx, ny), 2)

    def moved_y(f, offset):
        rolled = pltpu.roll(f, (-offset) % ny, 2)
        keep = lane < ny - offset if offset > 0 else lane >= -offset
        return jnp.where(keep, rolled, 0.0)

    def forward(f0, f1, f2, fm1):
        return coef_near * (f1 - f0) - coef_far * (f2 - fm1)

    def backward(f0, fm1, f1, fm2):
        return coef_near * (f0 - fm1) - coef_far * (f1 - fm2)

    loads[10].wait()
    loads[11].wait()
    for e in range(4):
        pack(1, 2 * e, item.at[e], item.at[e], 1, 2, 8)
        pack(1, 2 * e + 1, weight.at[e], weight.at[e], 1, 2, 8)
    start_sides(1)

    swap.wait_recv()
    first_core = comp == 0
    velocity = [jnp.where(first_core, own[k], other[k]) for k in range(3)]
    pressure, memory_fast, memory_slow = (
        jnp.where(first_core, other[k], own[k]) for k in range(3)
    )
    pack(0, 0, pressure, pressure, P_LAYERS, P_LAYERS)
    pack(0, P_LAYERS, velocity[0], velocity[1], 1, 2)
    start_sides(0)

    each_brick(lambda d: table_copy(d).wait_recv())
    lane_row = lax.broadcasted_iota(jnp.int32, (8, LANES), 1)
    per = LANES // CAP

    def brick_table(brick):
        chunk, first = brick // per, lax.rem(brick, per) * CAP
        rows = []
        for c in range(chunks):
            total = jnp.zeros((8, LANES), jnp.float32)
            for k in range(per):
                tile = table_recv[c * per + k, chunk]
                turned = pltpu.roll(tile, lax.rem(k * CAP - first + LANES, LANES), 1)
                total = jnp.where(
                    (lane_row >= k * CAP) & (lane_row < (k + 1) * CAP), turned, total
                )
            rows.append(total)
        return rows

    def lookup(rows, r, index):
        found = jnp.zeros(index.shape, jnp.float32)
        for c in range(chunks):
            source = jnp.broadcast_to(rows[c][r : r + 1], (index.shape[0], LANES))
            got = jnp.take_along_axis(
                source, lax.rem(index, LANES), axis=1, mode="promise_in_bounds"
            )
            found = got if chunks == 1 else jnp.where(index // LANES == c, got, found)
        return found

    own_rows = brick_table(me)

    def remap(r):
        return jnp.stack(
            [
                sum(weight[e, z] * lookup(own_rows, r, item[e, z]) for e in range(4))
                for z in range(nz)
            ]
        )

    weight_sum = weight[0] + weight[1] + weight[2] + weight[3]
    rd = courant * weight_sum / remap(1)
    bulk = courant * remap(0) / weight_sum
    gain = remap(2) / weight_sum
    gain_fast = (1.0 - decay_fast) * gain
    gain_slow = (1.0 - decay_slow) * gain

    def halo_rd(side):
        axis, step = SIDES[side]
        recv = (z_recv, x_recv)[side // 2]
        there = {**here, axis: jnp.where(exists(side), here[axis] + step, here[axis])}
        rows = brick_table(there["horiz"] * n_depth + there["depth"])
        found = []
        for k in range(V_LAYERS[side ^ 1]):
            total, scale = 0.0, 0.0
            for e in range(4):
                index = recv[1, side % 2, 8 * k + 2 * e].astype(jnp.int32)
                share = recv[1, side % 2, 8 * k + 2 * e + 1]
                total = total + share * lookup(rows, 1, index)
                scale = scale + share
            found.append(jnp.where(exists(side), courant * scale / total, 0.0))
        return found

    def fill_p(message):
        for k in range(P_LAYERS):
            p_x[:, k, :] = x_recv[message, 0, k]
            p_x[:, P_LAYERS + nx + k, :] = x_recv[message, 1, k]

    span = v_x.shape[1]
    v_x[...] = jnp.zeros_like(v_x)
    rd_x[...] = jnp.zeros_like(rd_x)
    p_x[...] = jnp.zeros_like(p_x)

    wait_sides(0)
    v_x[:, 2 : 2 + nx, :] = velocity[1]
    for k in range(2):
        v_x[:, k, :] = x_recv[0, 0, P_LAYERS + k]
    v_x[:, 2 + nx, :] = x_recv[0, 1, P_LAYERS]
    vz_low, vz_high = z_recv[0, 0, P_LAYERS : P_LAYERS + 2], z_recv[0, 1, P_LAYERS : P_LAYERS + 1]
    v_z = jnp.concatenate([vz_low, velocity[0], vz_high], axis=0)
    v_y = velocity[2]
    rd_x[:, 2 : 2 + nx, :] = rd

    for step in range(STEPS):
        message = 0 if step == 0 else 1 + step
        p_x[:, P_LAYERS : P_LAYERS + nx, :] = pressure
        v_y = v_y - rd * forward(
            pressure, moved_y(pressure, 1), moved_y(pressure, 2), moved_y(pressure, -1)
        )
        part_y = backward(v_y, moved_y(v_y, -1), moved_y(v_y, 1), moved_y(v_y, -2))
        if step == 0:
            wait_sides(1)
            halos = [halo_rd(side) for side in range(4)]
            for k in range(2):
                rd_x[:, k, :] = halos[2][k]
            rd_x[:, 2 + nx, :] = halos[3][0]
            rd_z = jnp.concatenate([jnp.stack(halos[0]), rd, jnp.stack(halos[1])], axis=0)
        if step > 0:
            wait_sides(message, (2, 3))
        fill_p(message)
        v_x[...] = v_x[...] - rd_x[...] * forward(
            p_x[:, 1 : 1 + span, :],
            p_x[:, 2 : 2 + span, :],
            p_x[:, 3 : 3 + span, :],
            p_x[:, 0:span, :],
        )
        part_x = backward(
            v_x[:, 2 : 2 + nx, :],
            v_x[:, 1 : 1 + nx, :],
            v_x[:, 3 : 3 + nx, :],
            v_x[:, 0:nx, :],
        )
        if step > 0:
            wait_sides(message, (0, 1))
        p_z = jnp.concatenate(
            [z_recv[message, 0, 0:P_LAYERS], pressure, z_recv[message, 1, 0:P_LAYERS]], axis=0
        )
        n = nz + 3
        v_z = v_z - rd_z * forward(
            p_z[1 : 1 + n], p_z[2 : 2 + n], p_z[3 : 3 + n], p_z[0:n]
        )
        part_z = backward(
            v_z[2 : 2 + nz], v_z[1 : 1 + nz], v_z[3 : 3 + nz], v_z[0:nz]
        )
        change = bulk * (part_z + part_x + part_y)
        memory_fast = decay_fast * memory_fast + gain_fast * change
        memory_slow = decay_slow * memory_slow + gain_slow * change
        pressure = pressure - change + memory_fast + memory_slow
        if step < STEPS - 1:
            pack(2 + step, 0, pressure, pressure, P_LAYERS, P_LAYERS)
            start_sides(2 + step)
            if step == 0:
                each_brick(lambda d: table_copy(d).wait_send())
                swap.wait_send()
                wait_sent(0)
            wait_sent(1 + step)

    out_ref[0, 0] = jnp.where(first_core, v_z[2 : 2 + nz], pressure)
    out_ref[0, 1] = jnp.where(first_core, v_x[:, 2 : 2 + nx, :], memory_fast)
    out_ref[0, 2] = jnp.where(first_core, v_y, memory_slow)

    wait_sent(MESSAGES - 1)


def per_device(
    co2_sat,
    pore_press,
    porosity,
    facies,
    destination,
    mineral_mod,
    dry_frac,
    grain_dens,
    relax_gain,
    intersection_item,
    intersection_weight,
    wave_state,
):
    bricks = lax.axis_size(("horiz", "depth"))
    cells = destination.shape[0]
    nz, nx, ny = intersection_item.shape[1:]
    chunks = bricks * CAP // LANES
    span = 8 * -(-(nx + 3) // 8)
    layers = max(P_LAYERS + 2, 8 * max(V_LAYERS))
    rows = [v.reshape(1, cells) for v in (co2_sat, pore_press, porosity, facies, destination)]
    f32 = jnp.float32
    return pl.pallas_call(
        kernel,
        out_shape=jax.ShapeDtypeStruct(wave_state.shape, f32),
        in_specs=[pl.BlockSpec(memory_space=pltpu.HBM)] * 12,
        out_specs=pl.BlockSpec(memory_space=pltpu.VMEM),
        scratch_shapes=[
            pltpu.VMEM((3, 1, cells), f32),
            pltpu.VMEM((2, 1, cells), jnp.int32),
            pltpu.SMEM((4, mineral_mod.shape[0]), f32),
            pltpu.VMEM(intersection_item.shape, jnp.int32),
            pltpu.VMEM(intersection_weight.shape, f32),
            pltpu.VMEM((3, nz, nx, ny), f32),
            pltpu.VMEM((3, nz, nx, ny), f32),
            pltpu.VMEM((chunks, 8, LANES), f32),
            pltpu.VMEM((bricks, chunks, 8, LANES), f32),
            pltpu.VMEM((MESSAGES, 2, layers, nx, ny), f32),
            pltpu.VMEM((MESSAGES, 2, layers, nz, ny), f32),
            pltpu.VMEM((MESSAGES, 2, layers, nx, ny), f32),
            pltpu.VMEM((MESSAGES, 2, layers, nz, ny), f32),
            pltpu.VMEM((nz, span + 8, ny), f32),
            pltpu.VMEM((nz, span, ny), f32),
            pltpu.VMEM((nz, span, ny), f32),
            pltpu.SemaphoreType.DMA((12,)),
            pltpu.SemaphoreType.DMA((2,)),
            pltpu.SemaphoreType.DMA((bricks,)),
            pltpu.SemaphoreType.DMA((bricks,)),
            pltpu.SemaphoreType.DMA((MESSAGES, 4)),
            pltpu.SemaphoreType.DMA((MESSAGES, 4)),
        ],
        compiler_params=pltpu.CompilerParams(
            collective_id=0, has_side_effects=True, vmem_limit_bytes=55040 * 1024
        ),
        name="remap_and_steps",
    )(
        *rows,
        mineral_mod,
        dry_frac,
        grain_dens,
        relax_gain,
        intersection_item,
        intersection_weight,
        wave_state,
    )


def solution(mesh):
    in_specs = (
        P(("parts", "horiz", "depth")),
        P(("parts", "horiz", "depth")),
        P(("parts", "horiz", "depth")),
        P(("parts", "horiz", "depth")),
        P(("parts", "horiz", "depth")),
        P(),
        P(),
        P(),
        P(),
        P(None, ("parts", "depth"), "horiz", None),
        P(None, ("parts", "depth"), "horiz", None),
        P("comp", None, ("parts", "depth"), "horiz", None),
    )
    out_specs = P("comp", None, ("parts", "depth"), "horiz", None)
    return jax.shard_map(
        per_device, mesh=mesh, in_specs=in_specs, out_specs=out_specs, check_vma=False
    )
```

```python
import functools

import jax
import jax.numpy as jnp
from jax import lax
from jax.experimental import pallas as pl
from jax.experimental.pallas import tpu as pltpu
from jax.sharding import PartitionSpec as P

STEPS = 4
CAP = 16
LANES = 128
MESH = pl.DeviceIdType.MESH

coef_near = 9.0 / 8.0
coef_far = 1.0 / 24.0
courant = 0.08
brine_modulus = 2.5
brine_density = 1.03
gas_density = 0.7
gas_base = 0.02
gas_slope = 0.1
decay_fast = 0.5
decay_slow = 0.9

SIDES = (("depth", -1), ("depth", 1), ("horiz", -1), ("horiz", 1))
P_LAYERS = 3
V_LAYERS = (1, 2, 1, 2)
MESSAGES = 2 + STEPS - 1


def rock_moduli(saturation, pressure_in, porous, k_min, dry_part, grain_rho):
    water_share = 1.0 - saturation
    k_gas = gas_base + gas_slope * pressure_in
    k_fluid = (brine_modulus - k_gas) * (water_share * water_share * water_share) + k_gas
    k_dry = dry_part * k_min * (1.0 - porous)
    dry_ratio = 1.0 - k_dry / k_min
    denominator = porous / k_fluid + (1.0 - porous) / k_min - k_dry / (k_min * k_min)
    k_sat = k_dry + dry_ratio * dry_ratio / denominator
    density = (1.0 - porous) * grain_rho + porous * (
        brine_density * water_share + gas_density * saturation
    )
    return k_sat, density


def kernel(
    sat_hbm,
    press_hbm,
    poro_hbm,
    facies_hbm,
    dest_hbm,
    mineral_hbm,
    dry_hbm,
    grain_hbm,
    relax_hbm,
    item_hbm,
    weight_hbm,
    state_hbm,
    out_ref,
    cells_f,
    cells_i,
    tables,
    item,
    weight,
    own,
    other,
    table_send,
    table_recv,
    z_send,
    x_send,
    z_recv,
    x_recv,
    p_x,
    v_x,
    rd_x,
    local_sem,
    partner_sem,
    table_send_sem,
    table_recv_sem,
    side_send_sem,
    side_recv_sem,
):
    horiz, depth, comp = (lax.axis_index(a) for a in ("horiz", "depth", "comp"))
    n_horiz, n_depth = lax.axis_size("horiz"), lax.axis_size("depth")
    bricks = n_horiz * n_depth
    me = horiz * n_depth + depth
    cells = dest_hbm.shape[1]
    facies_count = mineral_hbm.shape[0]
    nz, nx, ny = item.shape[1:]
    chunks = table_send.shape[0]
    here = {"depth": depth, "horiz": horiz}
    extent = {"depth": n_depth, "horiz": n_horiz}

    barrier = pltpu.get_barrier_semaphore()

    def brick_id(q):
        return {"horiz": q // n_depth, "depth": lax.rem(q, n_depth)}

    partner = {"comp": 1 - comp}

    def exists(side):
        axis, step = SIDES[side]
        place = here[axis] + step
        return (place >= 0) & (place < extent[axis])

    for side in range(4):

        @pl.when(jnp.logical_not(exists(side)))
        def _(side=side):
            halo = (z_recv, x_recv)[side // 2]
            for message in range(MESSAGES):
                rows = halo.shape[2] if message == 1 else P_LAYERS + 2
                halo[message, side % 2, 0:rows] = jnp.zeros((rows,) + halo.shape[3:], jnp.float32)

    def each_brick(body):
        if bricks <= 16:
            for d in range(1, bricks):
                body(d)
        else:
            lax.fori_loop(1, bricks, lambda d, c: (body(d), c)[1], 0)

    def greet(d):
        pl.semaphore_signal(
            barrier, inc=1, device_id=brick_id(lax.rem(me + d, bricks)), device_id_type=MESH
        )

    each_brick(greet)
    pl.semaphore_signal(barrier, inc=1, device_id=partner, device_id_type=MESH)

    sources = (
        (sat_hbm, cells_f.at[0]),
        (press_hbm, cells_f.at[1]),
        (poro_hbm, cells_f.at[2]),
        (facies_hbm, cells_i.at[0]),
        (dest_hbm, cells_i.at[1]),
        (mineral_hbm, tables.at[0]),
        (dry_hbm, tables.at[1]),
        (grain_hbm, tables.at[2]),
        (relax_hbm, tables.at[3]),
        (state_hbm.at[0], own),
        (item_hbm, item),
        (weight_hbm, weight),
    )
    loads = [
        pltpu.make_async_copy(src, dst, local_sem.at[k]) for k, (src, dst) in enumerate(sources)
    ]
    for load in loads:
        load.start()
    for load in loads[:9]:
        load.wait()

    facies = cells_i[0]
    drow = cells_i[1]
    picked = []
    for t in range(4):
        row = jnp.zeros(facies.shape, jnp.float32)
        for k in range(facies_count):
            row = jnp.where(facies == k, tables[t, k], row)
        picked.append(row)
    k_sat, rho = rock_moduli(cells_f[0], cells_f[1], cells_f[2], *picked[:3])
    row_id = lax.broadcasted_iota(jnp.int32, (8, cells), 0)
    moduli = jnp.where(
        row_id == 0, k_sat, jnp.where(row_id == 1, rho, jnp.where(row_id == 2, picked[3], 0.0))
    )
    high = moduli.astype(jnp.bfloat16)
    rest = moduli - high.astype(jnp.float32)
    middle = rest.astype(jnp.bfloat16)
    low = (rest - middle.astype(jnp.float32)).astype(jnp.bfloat16)
    pieces = jnp.concatenate(
        [high.astype(jnp.float32), middle.astype(jnp.float32), low.astype(jnp.float32)], axis=0
    ).astype(jnp.bfloat16)
    width = bricks * CAP
    group = min(cells, LANES)
    placed = jnp.zeros((24, width), jnp.float32)
    for first in range(0, cells, group):
        down = lax.broadcasted_iota(jnp.int32, (group, cells), 0) + first
        along = lax.broadcasted_iota(jnp.int32, (group, cells), 1)
        drow_f = drow.astype(jnp.float32)
        spread = jnp.broadcast_to(drow_f, (group, cells))
        dcol = jnp.sum(jnp.where(down == along, spread, 0.0), axis=1, keepdims=True)
        rank = jnp.sum(
            jnp.where((spread == dcol) & (along < down), 1.0, 0.0), axis=1, keepdims=True
        )
        slot = dcol * CAP + rank
        target = lax.broadcasted_iota(jnp.int32, (group, width), 1).astype(jnp.float32)
        place = jnp.where(slot == target, 1.0, 0.0).astype(jnp.bfloat16)
        placed = placed + jnp.dot(
            pieces[:, first : first + group], place, preferred_element_type=jnp.float32
        )
    table = placed[0:8] + placed[8:16] + placed[16:24]
    for c in range(chunks):
        table_send[c] = table[:, c * LANES : (c + 1) * LANES]

    pl.semaphore_wait(barrier, bricks)

    def table_copy(d):
        return pltpu.make_async_remote_copy(
            src_ref=table_send,
            dst_ref=table_recv.at[me],
            send_sem=table_send_sem.at[d],
            recv_sem=table_recv_sem.at[d],
            device_id=brick_id(lax.rem(me + d, bricks)),
            device_id_type=MESH,
        )

    each_brick(lambda d: table_copy(d).start())
    loads[9].wait()
    swap = pltpu.make_async_remote_copy(
        src_ref=own,
        dst_ref=other,
        send_sem=partner_sem.at[0],
        recv_sem=partner_sem.at[1],
        device_id=partner,
        device_id_type=MESH,
    )
    swap.start()
    table_recv[me] = table_send[...]

    def side_copy(message, side, rows, arriving=False):
        axis, step = SIDES[side]
        send, recv = (z_send, z_recv) if axis == "depth" else (x_send, x_recv)
        mine, theirs = side % 2, (side % 2) ^ 1
        return pltpu.make_async_remote_copy(
            src_ref=send.at[message, mine, pl.ds(0, rows)],
            dst_ref=recv.at[message, theirs, pl.ds(0, rows)],
            send_sem=side_send_sem.at[message, side],
            recv_sem=side_recv_sem.at[message, side ^ 1],
            device_id={axis: here[axis] + (-step if arriving else step)},
            device_id_type=MESH,
        )

    def rows_of(message, side):
        if message == 0:
            return P_LAYERS + V_LAYERS[side]
        return 8 * V_LAYERS[side] if message == 1 else P_LAYERS

    def start_sides(message):
        for side in (2, 3, 0, 1):

            @pl.when(exists(side))
            def _(side=side):
                side_copy(message, side, rows_of(message, side)).start()

    def wait_sides(message, sides=(2, 3, 0, 1)):
        for side in sides:

            @pl.when(exists(side))
            def _(side=side):
                side_copy(message, side ^ 1, rows_of(message, side ^ 1), True).wait_recv()

    def wait_sent(message):
        for side in range(4):

            @pl.when(exists(side))
            def _(side=side):
                side_copy(message, side, rows_of(message, side)).wait_send()

    def pack(message, first, along_z, along_x, layers_low, layers_high, apart=1):
        for k in range(layers_low):
            z_send[message, 0, first + apart * k] = along_z[k].astype(jnp.float32)
            x_send[message, 0, first + apart * k] = along_x[:, k, :].astype(jnp.float32)
        for k in range(layers_high):
            layer_z, layer_x = nz - layers_high + k, nx - layers_high + k
            z_send[message, 1, first + apart * k] = along_z[layer_z].astype(jnp.float32)
            x_send[message, 1, first + apart * k] = along_x[:, layer_x, :].astype(jnp.float32)

    lane = lax.broadcasted_iota(jnp.int32, (nz, nx, ny), 2)

    def moved_y(f, offset):
        rolled = pltpu.roll(f, (-offset) % ny, 2)
        keep = lane < ny - offset if offset > 0 else lane >= -offset
        return jnp.where(keep, rolled, 0.0)

    def forward(f0, f1, f2, fm1):
        return coef_near * (f1 - f0) - coef_far * (f2 - fm1)

    def backward(f0, fm1, f1, fm2):
        return coef_near * (f0 - fm1) - coef_far * (f1 - fm2)

    loads[10].wait()
    loads[11].wait()
    for e in range(4):
        pack(1, 2 * e, item.at[e], item.at[e], 1, 2, 8)
        pack(1, 2 * e + 1, weight.at[e], weight.at[e], 1, 2, 8)
    start_sides(1)

    swap.wait_recv()
    first_core = comp == 0
    velocity = [jnp.where(first_core, own[k], other[k]) for k in range(3)]
    pressure, memory_fast, memory_slow = (
        jnp.where(first_core, other[k], own[k]) for k in range(3)
    )
    pack(0, 0, pressure, pressure, P_LAYERS, P_LAYERS)
    pack(0, P_LAYERS, velocity[0], velocity[1], 1, 2)
    start_sides(0)

    each_brick(lambda d: table_copy(d).wait_recv())
    lane_row = lax.broadcasted_iota(jnp.int32, (8, LANES), 1)
    per = LANES // CAP

    def brick_table(brick):
        chunk, first = brick // per, lax.rem(brick, per) * CAP
        rows = []
        for c in range(chunks):
            total = jnp.zeros((8, LANES), jnp.float32)
            for k in range(per):
                tile = table_recv[c * per + k, chunk]
                turned = pltpu.roll(tile, lax.rem(k * CAP - first + LANES, LANES), 1)
                total = jnp.where(
                    (lane_row >= k * CAP) & (lane_row < (k + 1) * CAP), turned, total
                )
            rows.append(total)
        return rows

    def lookup(rows, r, index):
        found = jnp.zeros(index.shape, jnp.float32)
        for c in range(chunks):
            source = jnp.broadcast_to(rows[c][r : r + 1], (index.shape[0], LANES))
            got = jnp.take_along_axis(
                source, lax.rem(index, LANES), axis=1, mode="promise_in_bounds"
            )
            found = got if chunks == 1 else jnp.where(index // LANES == c, got, found)
        return found

    own_rows = brick_table(me)

    def remap(r):
        return jnp.stack(
            [
                sum(weight[e, z] * lookup(own_rows, r, item[e, z]) for e in range(4))
                for z in range(nz)
            ]
        )

    weight_sum = weight[0] + weight[1] + weight[2] + weight[3]
    rd = courant * weight_sum / remap(1)
    bulk = courant * remap(0) / weight_sum
    gain = remap(2) / weight_sum
    gain_fast = (1.0 - decay_fast) * gain
    gain_slow = (1.0 - decay_slow) * gain

    def halo_rd(side):
        axis, step = SIDES[side]
        recv = (z_recv, x_recv)[side // 2]
        there = {**here, axis: jnp.where(exists(side), here[axis] + step, here[axis])}
        rows = brick_table(there["horiz"] * n_depth + there["depth"])
        found = []
        for k in range(V_LAYERS[side ^ 1]):
            total, scale = 0.0, 0.0
            for e in range(4):
                index = recv[1, side % 2, 8 * k + 2 * e].astype(jnp.int32)
                share = recv[1, side % 2, 8 * k + 2 * e + 1]
                total = total + share * lookup(rows, 1, index)
                scale = scale + share
            found.append(jnp.where(exists(side), courant * scale / total, 0.0))
        return found

    def fill_p(message):
        for k in range(P_LAYERS):
            p_x[:, k, :] = x_recv[message, 0, k]
            p_x[:, P_LAYERS + nx + k, :] = x_recv[message, 1, k]

    span = v_x.shape[1]
    v_x[...] = jnp.zeros_like(v_x)
    rd_x[...] = jnp.zeros_like(rd_x)
    p_x[...] = jnp.zeros_like(p_x)

    wait_sides(0)
    v_x[:, 2 : 2 + nx, :] = velocity[1]
    for k in range(2):
        v_x[:, k, :] = x_recv[0, 0, P_LAYERS + k]
    v_x[:, 2 + nx, :] = x_recv[0, 1, P_LAYERS]
    vz_low, vz_high = z_recv[0, 0, P_LAYERS : P_LAYERS + 2], z_recv[0, 1, P_LAYERS : P_LAYERS + 1]
    v_z = jnp.concatenate([vz_low, velocity[0], vz_high], axis=0)
    v_y = velocity[2]
    rd_x[:, 2 : 2 + nx, :] = rd

    for step in range(STEPS):
        message = 0 if step == 0 else 1 + step
        p_x[:, P_LAYERS : P_LAYERS + nx, :] = pressure
        v_y = v_y - rd * forward(
            pressure, moved_y(pressure, 1), moved_y(pressure, 2), moved_y(pressure, -1)
        )
        part_y = backward(v_y, moved_y(v_y, -1), moved_y(v_y, 1), moved_y(v_y, -2))
        if step == 0:
            wait_sides(1)
            halos = [halo_rd(side) for side in range(4)]
            for k in range(2):
                rd_x[:, k, :] = halos[2][k]
            rd_x[:, 2 + nx, :] = halos[3][0]
            rd_z = jnp.concatenate([jnp.stack(halos[0]), rd, jnp.stack(halos[1])], axis=0)
        if step > 0:
            wait_sides(message, (2, 3))
        fill_p(message)
        v_x[...] = v_x[...] - rd_x[...] * forward(
            p_x[:, 1 : 1 + span, :],
            p_x[:, 2 : 2 + span, :],
            p_x[:, 3 : 3 + span, :],
            p_x[:, 0:span, :],
        )
        part_x = backward(
            v_x[:, 2 : 2 + nx, :],
            v_x[:, 1 : 1 + nx, :],
            v_x[:, 3 : 3 + nx, :],
            v_x[:, 0:nx, :],
        )
        if step > 0:
            wait_sides(message, (0, 1))
        p_z = jnp.concatenate(
            [z_recv[message, 0, 0:P_LAYERS], pressure, z_recv[message, 1, 0:P_LAYERS]], axis=0
        )
        n = nz + 3
        v_z = v_z - rd_z * forward(
            p_z[1 : 1 + n], p_z[2 : 2 + n], p_z[3 : 3 + n], p_z[0:n]
        )
        part_z = backward(
            v_z[2 : 2 + nz], v_z[1 : 1 + nz], v_z[3 : 3 + nz], v_z[0:nz]
        )
        change = bulk * (part_z + part_x + part_y)
        memory_fast = decay_fast * memory_fast + gain_fast * change
        memory_slow = decay_slow * memory_slow + gain_slow * change
        pressure = pressure - change + memory_fast + memory_slow
        if step < STEPS - 1:
            pack(2 + step, 0, pressure, pressure, P_LAYERS, P_LAYERS)
            start_sides(2 + step)
            if step == 0:
                each_brick(lambda d: table_copy(d).wait_send())
                swap.wait_send()
                wait_sent(0)
            wait_sent(1 + step)

    out_ref[0, 0] = jnp.where(first_core, v_z[2 : 2 + nz], pressure)
    out_ref[0, 1] = jnp.where(first_core, v_x[:, 2 : 2 + nx, :], memory_fast)
    out_ref[0, 2] = jnp.where(first_core, v_y, memory_slow)

    wait_sent(MESSAGES - 1)


def per_device(
    co2_sat,
    pore_press,
    porosity,
    facies,
    destination,
    mineral_mod,
    dry_frac,
    grain_dens,
    relax_gain,
    intersection_item,
    intersection_weight,
    wave_state,
):
    bricks = lax.axis_size(("horiz", "depth"))
    cells = destination.shape[0]
    nz, nx, ny = intersection_item.shape[1:]
    chunks = bricks * CAP // LANES
    span = 8 * -(-(nx + 3) // 8)
    layers = max(P_LAYERS + 2, 8 * max(V_LAYERS))
    rows = [v.reshape(1, cells) for v in (co2_sat, pore_press, porosity, facies, destination)]
    f32 = jnp.float32
    return pl.pallas_call(
        kernel,
        out_shape=jax.ShapeDtypeStruct(wave_state.shape, f32),
        in_specs=[pl.BlockSpec(memory_space=pltpu.HBM)] * 12,
        out_specs=pl.BlockSpec(memory_space=pltpu.VMEM),
        scratch_shapes=[
            pltpu.VMEM((3, 1, cells), f32),
            pltpu.VMEM((2, 1, cells), jnp.int32),
            pltpu.SMEM((4, mineral_mod.shape[0]), f32),
            pltpu.VMEM(intersection_item.shape, jnp.int32),
            pltpu.VMEM(intersection_weight.shape, f32),
            pltpu.VMEM((3, nz, nx, ny), f32),
            pltpu.VMEM((3, nz, nx, ny), f32),
            pltpu.VMEM((chunks, 8, LANES), f32),
            pltpu.VMEM((bricks, chunks, 8, LANES), f32),
            pltpu.VMEM((MESSAGES, 2, layers, nx, ny), f32),
            pltpu.VMEM((MESSAGES, 2, layers, nz, ny), f32),
            pltpu.VMEM((MESSAGES, 2, layers, nx, ny), f32),
            pltpu.VMEM((MESSAGES, 2, layers, nz, ny), f32),
            pltpu.VMEM((nz, span + 8, ny), f32),
            pltpu.VMEM((nz, span, ny), f32),
            pltpu.VMEM((nz, span, ny), f32),
            pltpu.SemaphoreType.DMA((12,)),
            pltpu.SemaphoreType.DMA((2,)),
            pltpu.SemaphoreType.DMA((bricks,)),
            pltpu.SemaphoreType.DMA((bricks,)),
            pltpu.SemaphoreType.DMA((MESSAGES, 4)),
            pltpu.SemaphoreType.DMA((MESSAGES, 4)),
        ],
        compiler_params=pltpu.CompilerParams(
            collective_id=0, has_side_effects=True, vmem_limit_bytes=55040 * 1024
        ),
        name="remap_and_steps",
    )(
        *rows,
        mineral_mod,
        dry_frac,
        grain_dens,
        relax_gain,
        intersection_item,
        intersection_weight,
        wave_state,
    )


def solution(mesh):
    in_specs = (
        P(("parts", "horiz", "depth")),
        P(("parts", "horiz", "depth")),
        P(("parts", "horiz", "depth")),
        P(("parts", "horiz", "depth")),
        P(("parts", "horiz", "depth")),
        P(),
        P(),
        P(),
        P(),
        P(None, ("parts", "depth"), "horiz", None),
        P(None, ("parts", "depth"), "horiz", None),
        P("comp", None, ("parts", "depth"), "horiz", None),
    )
    out_specs = P("comp", None, ("parts", "depth"), "horiz", None)
    return jax.shard_map(
        per_device, mesh=mesh, in_specs=in_specs, out_specs=out_specs, check_vma=False
    )
```
